512 devices in a mesh: dp: 8 (over x, core), ctx: 64 (over y, z).
Axes of the slice: x: 4, y: 4, z: 16, core: 2. Of those that a mesh axis runs over, the one named last changes fastest.
Arguments:
- queries: bfloat16 [131072, 2048], P(('dp', 'ctx')), may hold values from -5 to 5
- keys: bfloat16 [131072, 512], P(('dp', 'ctx')), may hold values from -5 to 5
- values: bfloat16 [131072, 512], P(('dp', 'ctx')), may hold values from -5 to 5
- grad_out: bfloat16 [131072, 2048], P(('dp', 'ctx')), may hold values from -5 to 5
- doc_lengths: int32 [341], replicated, may hold values from 1 to 768, 131072 in all
Outputs:
- grad_queries: bfloat16 [131072, 2048], P(('dp', 'ctx'))
- grad_keys: bfloat16 [131072, 512], P(('dp', 'ctx'))
- grad_values: bfloat16 [131072, 512], P(('dp', 'ctx'))
The draws below stay inside these ranges and needn't reach their ends.
Inputs may be any that keep to these rules, and one draw needn't show every extreme that they name: `doc_lengths`: they sum to 131072; the longest is exactly 768.
All inputs are finite; a program needn't handle non-finite values.
Results may differ from the reference program's by a relative error of at most 0.024.
Values may be sent and summed in bfloat16 or wider, within the bound.
No kernel may reach another device: no remote copies, remote signals or barrier semaphores. Data moves between devices by JAX's collectives and lax.ppermute only.
A program may use at most 64 MiB of HBM per device.

```python
import math
import jax
import jax.numpy as jnp
import numpy as np
from jax import lax

HEADS = 16
KV_HEADS = 4
HEAD_DIM = 128
REACH = 3
TOK_DEV = 256
LENGTH = 131072
DOCMAX = 768
DOCS = 341


def draw_queries(key, part):
    key = jax.random.fold_in(key, 7)
    return jax.random.truncated_normal(key, -4.5, 4.5, (LENGTH, HEADS * HEAD_DIM), jnp.float32).astype(jnp.bfloat16)


def draw_keys(key, part):
    key = jax.random.fold_in(key, 9)
    return jax.random.truncated_normal(key, -4.5, 4.5, (LENGTH, KV_HEADS * HEAD_DIM), jnp.float32).astype(jnp.bfloat16)


def level_of(own_key, shape, pieces, least, largest):
    def one(axis_at, parts):
        steps = jax.random.uniform(jax.random.fold_in(jax.random.fold_in(own_key, 6), axis_at), (parts,), jnp.float32, least / len(pieces), largest / len(pieces))
        return jnp.repeat(jnp.exp(steps), shape[axis_at] // parts).reshape((-1,) + (1,) * (len(shape) - axis_at - 1))

    level = one(*pieces[0])
    for cut in pieces[1:]:
        level = level * one(*cut)
    return level


def split_up(number_of, total, limit, skew):
    portions = [(1 << 20) // math.isqrt(grade ** skew) + 1 for grade in range(2, number_of + 1)]
    spare, counts = total - limit - (number_of - 1), [1] * (number_of - 1)
    while spare > 0:
        movable = [i for i in range(number_of - 1) if counts[i] < limit]
        whole, left = sum([portions[i] for i in movable]), spare
        for i in movable:
            extra = min(limit - counts[i], max(1, left * portions[i] // whole), spare)
            counts[i] = counts[i] + extra
            spare = spare - extra
    return np.array([limit] + counts)


def ragged_sizes(own_key, amount, total, limit, skew):
    if amount == 2:
        one = jax.random.randint(own_key, (), max(1, total - limit), min(limit, total - 1) + 1)
        return jnp.stack([one, total - one])
    lengths = jnp.asarray(split_up(amount, total, limit, skew), jnp.int32)
    pairs = (amount - 1) // 2
    giver, sink = lengths[1:1 + 2 * pairs:2], lengths[2:2 + 2 * pairs:2]
    room = jnp.minimum(giver - 1, limit - sink)
    shifted = jax.random.randint(jax.random.fold_in(own_key, 1), (pairs,), 0, 1 << 20) % (room + 1)
    lengths = lengths.at[1:1 + 2 * pairs:2].set(giver - shifted).at[2:2 + 2 * pairs:2].set(sink + shifted)
    return lengths[jax.random.permutation(jax.random.fold_in(own_key, 2), amount)]


def noise(rng, shape, deviation, reach, shards=(), held_as=jnp.bfloat16):
    array = jax.random.normal(rng, shape, jnp.float32) * deviation
    if len(shards) > 0:
        array = level_of(rng, shape, shards, -0.22, 0.18) * array
    return jnp.clip(array, min=-reach, max=reach).astype(held_as)


def setup_inputs(seed: int = 0) -> dict:
    splits = jax.random.split(jax.random.key(seed), 6)
    queries = draw_queries(jax.random.fold_in(splits[5], 71), 0)
    keys = draw_keys(jax.random.fold_in(splits[5], 71), 0)
    values = noise(splits[2], (LENGTH, KV_HEADS * HEAD_DIM), 1.0, 5.0, ((0, 512),))
    grad_out = noise(splits[3], (LENGTH, HEADS * HEAD_DIM), 1.0, 5.0, ((0, 512),))
    doc_lengths = ragged_sizes(splits[4], DOCS, LENGTH, DOCMAX, 2).astype(jnp.int32)
    return {"queries": queries, "keys": keys, "values": values, "grad_out": grad_out, "doc_lengths": doc_lengths}


def doc_mask(ends, q_pos, k_pos):
    q_doc = jnp.sum((ends[None, :] <= q_pos[:, None]).astype(jnp.int32), axis=1)
    k_doc = jnp.sum((ends[None, :] <= k_pos[:, None]).astype(jnp.int32), axis=1)
    return (q_doc[:, None] == k_doc[None, :]) & (k_pos[None, :] <= q_pos[:, None]) & (k_pos[None, :] >= 0)


def group_terms(q_group, k_group, v_group, g_group, allowed, scale):
    q_f = q_group.astype(jnp.float32)
    k_f = k_group.astype(jnp.float32)
    v_f = v_group.astype(jnp.float32)
    g_f = g_group.astype(jnp.float32)
    scores = jnp.einsum("tgd,kd->gtk", q_f, k_f) * scale
    masked = jnp.where(allowed[None], scores, -1e30)
    top = jnp.max(masked, axis=2, keepdims=True)
    expo = jnp.where(allowed[None], jnp.exp(masked - top), 0.0)
    probs = expo / jnp.sum(expo, axis=2, keepdims=True)
    probs_b = lax.optimization_barrier(probs.astype(jnp.bfloat16))
    attn = jnp.einsum("gtk,kd->tgd", probs_b.astype(jnp.float32), v_f).astype(jnp.bfloat16)
    attn = lax.optimization_barrier(attn)
    delta = jnp.einsum("tgd,tgd->gt", g_f, attn.astype(jnp.float32))
    dprobs = jnp.einsum("tgd,kd->gtk", g_f, v_f)
    dscores = lax.optimization_barrier((probs * (dprobs - delta[:, :, None])).astype(jnp.bfloat16))
    d_f = dscores.astype(jnp.float32)
    grad_q = (jnp.einsum("gtk,kd->tgd", d_f, k_f) * scale).astype(jnp.bfloat16)
    grad_k = jnp.einsum("gtk,tgd->kd", d_f, q_f) * scale
    grad_v = jnp.einsum("gtk,tgd->kd", probs_b.astype(jnp.float32), g_f)
    return grad_q, grad_k, grad_v


def block_terms(q_block, window, g_block, allowed):
    tok = q_block.shape[0]
    width = window.shape[0]
    groups = HEADS // KV_HEADS
    kv_width = KV_HEADS * HEAD_DIM
    scale = HEAD_DIM ** -0.5
    q_split = q_block.reshape(tok, KV_HEADS, groups, HEAD_DIM).transpose(1, 0, 2, 3)
    g_split = g_block.reshape(tok, KV_HEADS, groups, HEAD_DIM).transpose(1, 0, 2, 3)
    k_split = window[:, :kv_width].reshape(width, KV_HEADS, HEAD_DIM).transpose(1, 0, 2)
    v_split = window[:, kv_width:].reshape(width, KV_HEADS, HEAD_DIM).transpose(1, 0, 2)
    grad_q, grad_k, grad_v = lax.map(lambda xs: group_terms(xs[0], xs[1], xs[2], xs[3], allowed, scale), (q_split, k_split, v_split, g_split))
    grad_q = grad_q.transpose(1, 0, 2, 3).reshape(tok, HEADS * HEAD_DIM)
    grad_k = grad_k.transpose(1, 0, 2).reshape(width, kv_width)
    grad_v = grad_v.transpose(1, 0, 2).reshape(width, kv_width)
    return grad_q, jnp.concatenate([grad_k, grad_v], axis=1)


def reference(queries, keys, values, grad_out, doc_lengths):
    tok = TOK_DEV
    width = (REACH + 1) * tok
    blocks = LENGTH // tok
    kv_width = KV_HEADS * HEAD_DIM
    ends = jnp.cumsum(doc_lengths).astype(jnp.int32)
    packed = jnp.concatenate([keys, values], axis=1)
    padded = jnp.concatenate([jnp.zeros((REACH * tok, 2 * kv_width), jnp.bfloat16), packed], axis=0)

    def step(carry, block):
        start = (block * tok).astype(jnp.int32)
        q_block = lax.dynamic_slice_in_dim(queries, start, tok, 0)
        g_block = lax.dynamic_slice_in_dim(grad_out, start, tok, 0)
        window = lax.dynamic_slice_in_dim(padded, start, width, 0)
        q_pos = start + jnp.arange(tok, dtype=jnp.int32)
        k_pos = start - REACH * tok + jnp.arange(width, dtype=jnp.int32)
        allowed = doc_mask(ends, q_pos, k_pos)
        grad_q, grad_kv = block_terms(q_block, window, g_block, allowed)
        old = lax.dynamic_slice_in_dim(carry, start, width, 0)
        carry = lax.dynamic_update_slice_in_dim(carry, old + grad_kv, start, 0)
        return carry, grad_q

    carry = jnp.zeros(((blocks + REACH) * tok, 2 * kv_width), jnp.float32)
    final, grad_q = lax.scan(step, carry, jnp.arange(blocks, dtype=jnp.int32))
    grad_kv = final[REACH * tok:]
    grad_queries = grad_q.reshape(LENGTH, HEADS * HEAD_DIM)
    return grad_queries, grad_kv[:, :kv_width].astype(jnp.bfloat16), grad_kv[:, kv_width:].astype(jnp.bfloat16)
```

```python
import functools
import jax, jax.numpy as jnp
from jax import lax
from jax.sharding import PartitionSpec as P
from jax.experimental import pallas as pl
from jax.experimental.pallas import tpu as pltpu
HEAD_DIM=128; REACH=3; TOK=256; HALF=128; GROUP=4
LANES=GROUP*HALF
SCALE=HEAD_DIM**-0.5
LOG2E=1.4426950408889634
NEG=-1e30
F32=jnp.float32; BF=jnp.bfloat16
def nt(a,b): return lax.dot_general(a,b,(((1,),(1,)),((),())),preferred_element_type=F32)
def nn(a,b): return lax.dot_general(a,b,(((1,),(0,)),((),())),preferred_element_type=F32)
def fold(x,op):
    r=x[:8]
    for i in range(1,x.shape[0]//8): r=op(r,x[i*8:(i+1)*8])
    return r
def rows_of(d,hf):
    if d==0 and hf==0: return 0,128
    if d==3 and hf==1: return 128,256
    return 0,256
def kernel(before_ref,start_ref,q_ref,g_ref,kv0,kv1,kv2,kv3,gq_ref,o0,o1,o2,o3,q4,g4,s_ref,dp_ref,m_ref,l_ref,e_ref,acc_ref):
    kv=(kv0,kv1,kv2,kv3); outs=(o0,o1,o2,o3)
    before=before_ref[0]
    for hf in range(2):
        for h in range(GROUP):
            r=slice(hf*LANES+h*HALF,hf*LANES+(h+1)*HALF)
            q4[r,:]=q_ref[hf*HALF:(hf+1)*HALF,h*128:(h+1)*128]
            g4[r,:]=g_ref[hf*HALF:(hf+1)*HALF,h*128:(h+1)*128]
    def lanes(hf): return slice(hf*LANES,(hf+1)*LANES)
    def gate(d,f):
        if d==0: f()
        else: pl.when(before>(d-1)*TOK)(f)
    def pass1(d):
        for hf in range(2):
            a,b=rows_of(d,hf); ln=lanes(hf)
            s=nt(kv[d][a:b,:128],q4[ln,:])
            st=start_ref[:,hf*HALF:(hf+1)*HALF]
            kpos=lax.broadcasted_iota(jnp.int32,(b-a,HALF),0)+(a-d*TOK)
            ok=kpos>=st
            if d==0: ok=ok&(kpos<=lax.broadcasted_iota(jnp.int32,(b-a,HALF),1)+hf*HALF)
            s=jnp.concatenate([jnp.where(ok,s[:,h*HALF:(h+1)*HALF],NEG) for h in range(GROUP)],axis=1)
            s_ref[d,a:b,ln]=s
            mx=fold(s,jnp.maximum)
            m_ref[:,ln]=mx if d==0 else jnp.maximum(m_ref[:,ln],mx)
    for d in range(4): gate(d,functools.partial(pass1,d))
    m_ref[...]=jnp.broadcast_to(jnp.max(m_ref[...],axis=0,keepdims=True),m_ref.shape)
    def pass2(d):
        for hf in range(2):
            a,b=rows_of(d,hf); ln=lanes(hf)
            p=jnp.exp2((s_ref[d,a:b,ln]-m_ref[:1,ln])*(SCALE*LOG2E))
            dp=nt(kv[d][a:b,128:],g4[ln,:])
            s_ref[d,a:b,ln]=p
            dp_ref[d,a:b,ln]=dp
            ls=fold(p,jnp.add); es=fold(p*dp,jnp.add)
            l_ref[:,ln]=ls if d==0 else l_ref[:,ln]+ls
            e_ref[:,ln]=es if d==0 else e_ref[:,ln]+es
    for d in range(4): gate(d,functools.partial(pass2,d))
    il=1.0/jnp.sum(l_ref[...],axis=0,keepdims=True)
    l_ref[...]=jnp.broadcast_to(il,l_ref.shape)
    e_ref[...]=jnp.broadcast_to(jnp.sum(e_ref[...],axis=0,keepdims=True)*il,e_ref.shape)
    def pass3(d):
        dk=[];dv=[]
        for hf in range(2):
            a,b=rows_of(d,hf); ln=lanes(hf)
            pr=s_ref[d,a:b,ln]*l_ref[:1,ln]
            ds=(pr*(dp_ref[d,a:b,ln]-e_ref[:1,ln])).astype(BF)
            pb=pr.astype(BF)
            x=nn(ds,q4[ln,:])*SCALE; y=nn(pb,g4[ln,:])
            z=jnp.zeros((128,128),F32)
            if a: x=jnp.concatenate([z,x],0); y=jnp.concatenate([z,y],0)
            if b<256: x=jnp.concatenate([x,z],0); y=jnp.concatenate([y,z],0)
            dk.append(x); dv.append(y)
            kt=kv[d][a:b,:128].astype(F32).T.astype(BF)
            t=nn(kt,ds)
            if d==0: acc_ref[:,ln]=t
            else: acc_ref[:,ln]+=t
        outs[d][:,:128]=(dk[0]+dk[1]).astype(outs[d].dtype)
        outs[d][:,128:]=(dv[0]+dv[1]).astype(outs[d].dtype)
    for d in range(4):
        gate(d,functools.partial(pass3,d))
        if d:
            @pl.when(before<=(d-1)*TOK)
            def _(): outs[d][...]=jnp.zeros_like(outs[d])
    for hf in range(2):
        for h in range(GROUP):
            c=slice(hf*LANES+h*HALF,hf*LANES+(h+1)*HALF)
            gq_ref[hf*HALF:(hf+1)*HALF,h*128:(h+1)*128]=(acc_ref[:,c]*SCALE).T.astype(BF)
def call(before,start,q,g,kvs,ng,g0,interpret=False):
    col=lambda w:pl.BlockSpec((TOK,w),lambda i:(0,i))
    qcol=pl.BlockSpec((TOK,512),lambda i:(0,i+g0))
    return pl.pallas_call(kernel,grid=(ng,),
        in_specs=[pl.BlockSpec(memory_space=pltpu.SMEM),pl.BlockSpec((1,TOK),lambda i:(0,0)),qcol,qcol]+[col(256)]*4,
        out_specs=[col(512)]+[col(256)]*4,
        out_shape=[jax.ShapeDtypeStruct((TOK,512*ng),BF),jax.ShapeDtypeStruct((TOK,256*ng),F32)]+[jax.ShapeDtypeStruct((TOK,256*ng),BF)]*3,
        scratch_shapes=[pltpu.VMEM((1024,128),BF)]*2+[pltpu.VMEM((4,256,1024),F32)]*2+[pltpu.VMEM((8,1024),F32)]*3+[pltpu.VMEM((128,1024),F32)],
        compiler_params=pltpu.CompilerParams(vmem_limit_bytes=48*2**20),interpret=interpret)(before,start,q,g,*kvs)
CHUNKS = ((0, 2), (2, 2))


def pack_kernel(chunks, keys_ref, values_ref, *outs):
    for (first, count), out in zip(chunks, outs):
        for i in range(count):
            src = slice((first + i) * 128, (first + i + 1) * 128)
            out[:, i * 256 : i * 256 + 128] = keys_ref[:, src]
            out[:, i * 256 + 128 : i * 256 + 256] = values_ref[:, src]


def pack(keys, values, chunks):
    return pl.pallas_call(
        functools.partial(pack_kernel, chunks),
        out_shape=[jax.ShapeDtypeStruct((TOK, 256 * n), BF) for _, n in chunks],
    )(keys, values)


def final_kernel(chunks, *refs):
    own, got = refs[: len(chunks)], refs[len(chunks) : 2 * len(chunks)]
    gk, gv = refs[2 * len(chunks) :]
    for (first, count), a, b in zip(chunks, own, got):
        for i in range(count):
            dst = slice((first + i) * 128, (first + i + 1) * 128)
            k = slice(i * 256, i * 256 + 128)
            v = slice(i * 256 + 128, i * 256 + 256)
            gk[:, dst] = (a[:, k] + b[:, k].astype(F32)).astype(BF)
            gv[:, dst] = (a[:, v] + b[:, v].astype(F32)).astype(BF)


def final(own, got, chunks):
    return pl.pallas_call(
        functools.partial(final_kernel, chunks),
        out_shape=[jax.ShapeDtypeStruct((TOK, 512), BF)] * 2,
    )(*own, *got)


def shift(x, distance):
    devices = range(lax.axis_size(("dp", "ctx")))
    route = [(i - distance, i) for i in devices if i - distance in devices]
    return lax.ppermute(x, ("dp", "ctx"), route)


def add(a, b):
    return (a.astype(F32) + b.astype(F32)).astype(BF)


def on_device(queries, keys, values, grad_out, doc_lengths):
    first = lax.axis_index(("dp", "ctx")) * TOK
    ends = jnp.cumsum(doc_lengths)
    pos = first + jnp.arange(TOK, dtype=jnp.int32)
    starts = jnp.max(jnp.where(ends[:, None] <= pos[None, :], ends[:, None], 0), axis=0) - first
    before = jnp.maximum(-starts[:1], 0)
    windows = [[kv] for kv in pack(keys, values, CHUNKS)]
    for _ in range(REACH):
        for w in windows:
            w.append(shift(w[-1], 1))
    grads = [
        call(before, starts[None], queries, grad_out, w, n, f) for (f, n), w in zip(CHUNKS, windows)
    ]
    own = [g[1] for g in grads]
    got = [shift(g[4], -1) for g in grads]
    got = [shift(add(x, g[3]), -1) for x, g in zip(got, grads)]
    got = [shift(add(x, g[2]), -1) for x, g in zip(got, grads)]
    gk, gv = final(own, got, CHUNKS)
    gq = jnp.concatenate([g[0] for g in grads], axis=1)
    return gq, gk, gv


def solution(mesh):
    spec = P(("dp", "ctx"), None)
    return jax.shard_map(
        on_device,
        mesh=mesh,
        in_specs=(spec, spec, spec, spec, P()),
        out_specs=(spec, spec, spec),
        check_vma=False,
    )
```

```python
import functools

import jax
import jax.numpy as jnp
from jax import lax
from jax.experimental import pallas as pl
from jax.experimental.pallas import tpu as pltpu
from jax.sharding import PartitionSpec as P

HEAD_DIM = 128
REACH = 3
TOK = 256
HALF = 128
GROUP = 4
KV_HEADS = 4
LANES = GROUP * HALF
WIDE = 2 * LANES
SCALE = HEAD_DIM**-0.5
LOG2E = 1.4426950408889634
NEG = -1e30
F32 = jnp.float32
BF = jnp.bfloat16
VMEM_LIMIT = 16 * 2**20


def nt(a, b):
    return lax.dot_general(a, b, (((1,), (1,)), ((), ())), preferred_element_type=F32)


def nn(a, b):
    return lax.dot_general(a, b, (((1,), (0,)), ((), ())), preferred_element_type=F32)


def fold(x, op):
    total = x[:8]
    for i in range(1, x.shape[0] // 8):
        total = op(total, x[i * 8 : (i + 1) * 8])
    return total


def lanes(half):
    return slice(half * LANES, (half + 1) * LANES)


def rows_of(distance, half):
    if distance == 0 and half == 0:
        return 0, HALF
    if distance == REACH and half == 1:
        return HALF, TOK
    return 0, TOK


def regroup(dst, src):
    for half in range(2):
        for h in range(GROUP):
            at = half * LANES + h * HALF
            dst[at : at + HALF, :] = src[half * HALF : (half + 1) * HALF, h * 128 : (h + 1) * 128]


def masked_scores(distance, half, k, q4, start_ref):
    a, b = rows_of(distance, half)
    s = nt(k[a:b], q4[lanes(half), :])
    start = start_ref[:, half * HALF : (half + 1) * HALF]
    at = lax.broadcasted_iota(jnp.int32, (b - a, HALF), 0) + (a - distance * TOK)
    ok = at >= start
    if distance == 0:
        ok = ok & (at <= lax.broadcasted_iota(jnp.int32, (b - a, HALF), 1) + half * HALF)
    return jnp.concatenate(
        [jnp.where(ok, s[:, h * HALF : (h + 1) * HALF], NEG) for h in range(GROUP)], axis=1
    )


def local_probs(distance, k, q4, start_ref, p_ref, stat_ref):
    for half in range(2):
        a, b = rows_of(distance, half)
        ln = lanes(half)
        s = masked_scores(distance, half, k, q4, start_ref)
        top = jnp.max(fold(s, jnp.maximum), axis=0, keepdims=True)
        p = jnp.exp2((s - top) * (SCALE * LOG2E))
        p_ref[a:b, ln] = p.astype(BF)
        stat_ref[0:1, ln] = top
        stat_ref[1:2, ln] = jnp.sum(fold(p, jnp.add), axis=0, keepdims=True)


def local_dprobs(distance, v, g4, p_ref, dp_ref, sum_ref):
    for half in range(2):
        a, b = rows_of(distance, half)
        ln = lanes(half)
        dp = nt(v[a:b], g4[ln, :])
        dp_ref[a:b, ln] = dp
        sum_ref[0:1, ln] = jnp.sum(fold(p_ref[a:b, ln].astype(F32) * dp, jnp.add), axis=0, keepdims=True)


def joined(distance, halves):
    blank = jnp.zeros((HALF, HEAD_DIM), F32)
    full = []
    for half, x in enumerate(halves):
        a, b = rows_of(distance, half)
        x = jnp.concatenate([blank, x], 0) if a else x
        full.append(jnp.concatenate([x, blank], 0) if b < TOK else x)
    return full[0] + full[1]


def value_grad(distance, g4, p_ref, factor):
    halves = []
    for half in range(2):
        a, b = rows_of(distance, half)
        ln = lanes(half)
        probs = p_ref[a:b, ln].astype(F32) * factor[:, ln]
        halves.append(nn(probs.astype(BF), g4[ln, :]))
    return joined(distance, halves)


def key_query_grad(distance, k, q4, p_ref, dp_ref, factor, delta):
    dk, dq = [], []
    for half in range(2):
        a, b = rows_of(distance, half)
        ln = lanes(half)
        probs = p_ref[a:b, ln].astype(F32) * factor[:, ln]
        ds = (probs * (dp_ref[a:b, ln] - delta[:, ln])).astype(BF)
        dk.append(nn(ds, q4[ln, :]) * SCALE)
        dq.append(nn(k[a:b].astype(F32).T.astype(BF), ds))
    return joined(distance, dk), dq


def near(before_ref, distance):
    return before_ref[0] > (distance - 1) * TOK


def gated(distance, before_ref, work, other):
    if distance == 0:
        work()
    else:
        pl.when(near(before_ref, distance))(work)
        pl.when(jnp.logical_not(near(before_ref, distance)))(other)


def no_probs(stat_ref):
    stat_ref[0:1, :] = jnp.full((1, WIDE), NEG, F32)
    stat_ref[1:2, :] = jnp.zeros((1, WIDE), F32)


def probs_kernel(distance, before_ref, start_ref, q_ref, k_ref, *outs):
    i = pl.program_id(0)
    if distance == 0:
        q4_ref, p_ref, stat_ref = outs
        q4 = q4_ref.at[i]
        regroup(q4, q_ref)
    else:
        p_ref, stat_ref = outs
        q4 = q_ref.at[i]
    gated(
        distance,
        before_ref,
        lambda: local_probs(distance, k_ref[...], q4, start_ref, p_ref.at[i], stat_ref.at[i]),
        lambda: no_probs(stat_ref.at[i]),
    )


def dprobs_kernel(distance, before_ref, g_ref, v_ref, p_ref, *outs):
    i = pl.program_id(0)
    if distance == 0:
        g4_ref, dp_ref, sum_ref = outs
        g4 = g4_ref.at[i]
        regroup(g4, g_ref)
    else:
        dp_ref, sum_ref = outs
        g4 = g_ref.at[i]

    def other():
        sum_ref[i, 0:1, :] = jnp.zeros((1, WIDE), F32)

    gated(
        distance,
        before_ref,
        lambda: local_dprobs(distance, v_ref[...], g4, p_ref.at[i], dp_ref.at[i], sum_ref.at[i]),
        other,
    )


def far_value_kernel(before_ref, start_ref, q4_ref, g4_ref, k_ref, s0, s1, s2, part_ref, p_ref, row_ref, stat_ref):
    i = pl.program_id(0)
    row = row_ref.at[i]
    gated(
        REACH,
        before_ref,
        lambda: local_probs(REACH, k_ref[...], q4_ref.at[i], start_ref, p_ref.at[i], stat_ref),
        lambda: no_probs(stat_ref),
    )
    stats = (s0.at[i], s1.at[i], s2.at[i], stat_ref)
    top = functools.reduce(jnp.maximum, [s[0:1, :] for s in stats])
    weight = [jnp.exp2((s[0:1, :] - top) * (SCALE * LOG2E)) for s in stats]
    total = sum(w * s[1:2, :] for w, s in zip(weight, stats))
    for d in range(REACH + 1):
        row[d : d + 1, :] = weight[d] / total

    def work():
        part_ref[...] = value_grad(REACH, g4_ref.at[i], p_ref.at[i], row[REACH : REACH + 1, :]).astype(BF)

    def other():
        part_ref[...] = jnp.zeros_like(part_ref)

    gated(REACH, before_ref, work, other)


def far_key_kernel(before_ref, q4_ref, g4_ref, k_ref, v_ref, p_ref, row_ref, e0, e1, e2, part_ref, dq_ref, delta_ref, dp_ref, sum_ref):
    i = pl.program_id(0)
    row, dq_out = row_ref.at[i], dq_ref.at[i]

    def none():
        sum_ref[0:1, :] = jnp.zeros((1, WIDE), F32)

    gated(
        REACH,
        before_ref,
        lambda: local_dprobs(REACH, v_ref[...], g4_ref.at[i], p_ref.at[i], dp_ref, sum_ref),
        none,
    )
    sums = (e0.at[i], e1.at[i], e2.at[i], sum_ref)
    delta = sum(row[d : d + 1, :] * sums[d][0:1, :] for d in range(REACH + 1))
    delta_ref[i, 0:1, :] = delta

    def work():
        dk, dq = key_query_grad(
            REACH, k_ref[...], q4_ref.at[i], p_ref.at[i], dp_ref, row[REACH : REACH + 1, :], delta
        )
        part_ref[...] = dk.astype(BF)
        for half in range(2):
            dq_out[:, lanes(half)] = dq[half]

    def other():
        part_ref[...] = jnp.zeros_like(part_ref)
        dq_out[...] = jnp.zeros_like(dq_out)

    gated(REACH, before_ref, work, other)


def value_kernel(distance, before_ref, g4_ref, p_ref, row_ref, part_ref):
    i = pl.program_id(0)

    def work():
        factor = row_ref[i, distance : distance + 1, :]
        part_ref[...] = value_grad(distance, g4_ref.at[i], p_ref.at[i], factor).astype(part_ref.dtype)

    def other():
        part_ref[...] = jnp.zeros_like(part_ref)

    gated(distance, before_ref, work, other)


def key_kernel(distance, before_ref, q4_ref, k_ref, p_ref, dp_ref, row_ref, delta_ref, dq_in, part_ref, dq_ref):
    i = pl.program_id(0)
    dq_old = dq_in.at[i]

    def work():
        dk, dq = key_query_grad(
            distance,
            k_ref[...],
            q4_ref.at[i],
            p_ref.at[i],
            dp_ref.at[i],
            row_ref[i, distance : distance + 1, :],
            delta_ref[i, 0:1, :],
        )
        part_ref[...] = dk.astype(part_ref.dtype)
        for half in range(2):
            total = dq_old[:, lanes(half)] + dq[half]
            if distance:
                dq_ref[i, :, lanes(half)] = total
                continue
            total = total * SCALE
            for h in range(GROUP):
                dq_ref[half * HALF : (half + 1) * HALF, h * 128 : (h + 1) * 128] = (
                    total[:, h * HALF : (h + 1) * HALF].T.astype(BF)
                )

    def other():
        part_ref[...] = jnp.zeros_like(part_ref)
        dq_ref[i] = dq_old[...]

    gated(distance, before_ref, work, other)


SMEM = pl.BlockSpec(memory_space=pltpu.SMEM)
HELD = pl.BlockSpec(memory_space=pltpu.VMEM)
START = pl.BlockSpec((1, TOK), lambda i: (0, 0))
QUERY = pl.BlockSpec((TOK, GROUP * HEAD_DIM), lambda i: (0, i))
KEY = pl.BlockSpec((TOK, HEAD_DIM), lambda i: (0, i))


def held(rows, width, dtype):
    return HELD, pltpu.VMEM((KV_HEADS, rows, width), dtype)


GROUPED = held(WIDE, HEAD_DIM, BF)
PROBS = held(TOK, WIDE, BF)
DPROBS = held(TOK, WIDE, F32)
STATS = held(8, WIDE, F32)
QUERY_GRAD = held(HEAD_DIM, WIDE, F32)
PART = KEY, jax.ShapeDtypeStruct((TOK, KV_HEADS * HEAD_DIM), BF)
OWN = KEY, jax.ShapeDtypeStruct((TOK, KV_HEADS * HEAD_DIM), F32)
QUERY_OUT = QUERY, jax.ShapeDtypeStruct((TOK, KV_HEADS * GROUP * HEAD_DIM), BF)


def call(kernel, in_specs, outs, matmuls, args, scratch=()):
    return pl.pallas_call(
        kernel,
        grid=(KV_HEADS,),
        in_specs=in_specs,
        out_specs=[spec for spec, _ in outs],
        out_shape=[shape for _, shape in outs],
        scratch_shapes=scratch,
        compiler_params=pltpu.CompilerParams(vmem_limit_bytes=VMEM_LIMIT),
        cost_estimate=pl.CostEstimate(
            flops=matmuls * KV_HEADS * 2 * TOK * WIDE * HEAD_DIM, bytes_accessed=2**20, transcendentals=0
        ),
    )(*args)


def probs_of(distance, before, start, q, k):
    own = distance == 0
    return call(
        functools.partial(probs_kernel, distance),
        [SMEM, START, QUERY if own else HELD, KEY],
        [GROUPED] * own + [PROBS, STATS],
        1,
        (before, start, q, k),
    )


def dprobs_of(distance, before, g, v, p):
    own = distance == 0
    return call(
        functools.partial(dprobs_kernel, distance),
        [SMEM, QUERY if own else HELD, KEY, HELD],
        [GROUPED] * own + [DPROBS, STATS],
        1,
        (before, g, v, p),
    )


def far_value(before, start, q4, g4, k, *stats):
    return call(
        far_value_kernel,
        [SMEM, START, HELD, HELD, KEY, HELD, HELD, HELD],
        [PART, PROBS, STATS],
        2,
        (before, start, q4, g4, k, *stats),
        [pltpu.VMEM((8, WIDE), F32)],
    )


def far_key(before, q4, g4, k, v, p, row, *sums):
    return call(
        far_key_kernel,
        [SMEM, HELD, HELD, KEY, KEY] + [HELD] * 5,
        [PART, QUERY_GRAD, STATS],
        3,
        (before, q4, g4, k, v, p, row, *sums),
        [pltpu.VMEM((TOK, WIDE), F32), pltpu.VMEM((8, WIDE), F32)],
    )


def value_part(distance, before, g4, p, row):
    return call(
        functools.partial(value_kernel, distance),
        [SMEM, HELD, HELD, HELD],
        [PART if distance else OWN],
        1,
        (before, g4, p, row),
    )[0]


def key_part(distance, before, q4, k, p, dp, row, delta, dq):
    return call(
        functools.partial(key_kernel, distance),
        [SMEM, HELD, KEY] + [HELD] * 5,
        [PART, QUERY_GRAD] if distance else [OWN, QUERY_OUT],
        2,
        (before, q4, k, p, dp, row, delta, dq),
    )


def shift(x, distance):
    devices = range(lax.axis_size(("dp", "ctx")))
    route = [(i - distance, i) for i in devices if i - distance in devices]
    return lax.ppermute(x, ("dp", "ctx"), route)


def add(a, b):
    return (a.astype(F32) + b.astype(F32)).astype(BF)


def after(x, *others):
    return lax.optimization_barrier((x, *others))[0]


def in_hbm(x):
    return pltpu.with_memory_space_constraint(x, pltpu.HBM)


def on_device(queries, keys, values, grad_out, doc_lengths):
    first = lax.axis_index(("dp", "ctx")) * TOK
    ends = jnp.cumsum(doc_lengths)
    pos = first + jnp.arange(TOK, dtype=jnp.int32)
    start = jnp.max(jnp.where(ends[:, None] <= pos[None, :], ends[:, None], 0), axis=0) - first
    before = jnp.maximum(-start[:1], 0)
    start = start[None]
    k, v = [keys], [values]
    k.append(shift(k[0], 1))
    v.append(shift(after(values, start), 1))
    q4, p0, stat0 = probs_of(0, before, start, in_hbm(queries), in_hbm(keys))
    p, dp, stat, total = [p0], [], [stat0], []
    done = stat0
    for d in (1, 2):
        k[d] = after(k[d], done)
        k.append(shift(k[d], 1))
        x, y = probs_of(d, before, start, q4, k[d])
        p.append(x)
        stat.append(y)
        v[d] = after(v[d], y)
        v.append(shift(v[d], 1))
        if d == 1:
            late = after(grad_out, v[d])
            g4, dp0, sum0 = dprobs_of(0, before, in_hbm(late), in_hbm(values), p0)
            dp.append(dp0)
            total.append(sum0)
        x, y = dprobs_of(d, before, g4, v[d], p[d])
        dp.append(x)
        total.append(y)
        done = y
    k[3] = after(k[3], done)
    part, p3, row = far_value(before, start, q4, g4, k[3], *stat)
    gv = shift(part, -1)
    v[3] = after(v[3], part)
    part, dq, delta = far_key(before, q4, g4, k[3], v[3], p3, row, *total)
    gk = shift(part, -1)
    done = part
    for d in (2, 1):
        part = value_part(d, before, g4, p[d], after(row, done))
        gv = add(after(gv, part), part)
        done = gv
        gv = shift(gv, -1)
        part, dq = key_part(d, before, q4, k[d], p[d], dp[d], after(row, done), delta, dq)
        gk = add(after(gk, part), part)
        done = gk
        gk = shift(gk, -1)
    own_v = value_part(0, before, g4, p0, after(row, done))
    own_k, grad_queries = key_part(0, before, q4, keys, p0, dp0, after(row, own_v), delta, dq)
    gv = after(gv, own_k)
    return grad_queries, add(own_k, gk), add(own_v, gv)


def solution(mesh):
    spec = P(("dp", "ctx"), None)
    return jax.shard_map(
        on_device,
        mesh=mesh,
        in_specs=(spec, spec, spec, spec, P()),
        out_specs=(spec, spec, spec),
        check_vma=False,
    )
```

```python
import functools

import jax
import jax.numpy as jnp
from jax import lax
from jax.experimental import pallas as pl
from jax.experimental.pallas import tpu as pltpu
from jax.sharding import PartitionSpec as P

HEAD_DIM = 128
REACH = 3
TOK = 256
HALF = 128
GROUP = 4
KV_HEADS = 4
FAR_GROUPS = 2
LANES = GROUP * HALF
WIDE = 2 * LANES
SCALE = HEAD_DIM**-0.5
LOG2E = 1.4426950408889634
NEG = -1e30
F32 = jnp.float32
BF = jnp.bfloat16
VMEM_LIMIT = 20 * 2**20


def nt(a, b):
    return lax.dot_general(a, b, (((1,), (1,)), ((), ())), preferred_element_type=F32)


def nn(a, b):
    return lax.dot_general(a, b, (((1,), (0,)), ((), ())), preferred_element_type=F32)


def fold(x, op):
    total = x[:8]
    for i in range(1, x.shape[0] // 8):
        total = op(total, x[i * 8 : (i + 1) * 8])
    return total


def lanes(half):
    return slice(half * LANES, (half + 1) * LANES)


OWN_BLOCK, NEAR_BLOCK, LATE, EARLY = "own", "near", "late", "early"


def rows_of(case, half):
    if case == OWN_BLOCK and half == 0:
        return 0, HALF
    if case == LATE:
        return HALF, TOK
    if case == EARLY and half == 1:
        return 0, 0
    return 0, TOK


def halves_of(case):
    return [half for half in range(2) if rows_of(case, half)[1]]


def case_of(distance):
    return NEAR_BLOCK if distance else OWN_BLOCK


def regroup(dst, src):
    for half in range(2):
        for h in range(GROUP):
            at = half * LANES + h * HALF
            dst[at : at + HALF, :] = src[half * HALF : (half + 1) * HALF, h * 128 : (h + 1) * 128]


def masked_scores(case, distance, half, k, q4, start_ref):
    a, b = rows_of(case, half)
    s = nt(k[a:b], q4[lanes(half), :])
    start = start_ref[:, half * HALF : (half + 1) * HALF]
    at = lax.broadcasted_iota(jnp.int32, (b - a, HALF), 0) + (a - distance * TOK)
    ok = at >= start
    if case == OWN_BLOCK:
        ok = ok & (at <= lax.broadcasted_iota(jnp.int32, (b - a, HALF), 1) + half * HALF)
    return jnp.concatenate(
        [jnp.where(ok, s[:, h * HALF : (h + 1) * HALF], NEG) for h in range(GROUP)], axis=1
    )


def local_probs(case, distance, k, q4, start_ref, p_ref, stat_ref):
    if case == EARLY:
        no_probs(stat_ref)
    for half in halves_of(case):
        a, b = rows_of(case, half)
        ln = lanes(half)
        s = masked_scores(case, distance, half, k, q4, start_ref)
        top = jnp.max(fold(s, jnp.maximum), axis=0, keepdims=True)
        p = jnp.exp2((s - top) * (SCALE * LOG2E))
        p_ref[a:b, ln] = p.astype(BF)
        stat_ref[0:1, ln] = top
        stat_ref[1:2, ln] = jnp.sum(fold(p, jnp.add), axis=0, keepdims=True)


def local_dprobs(case, v, g4, p_ref, dp_ref, sum_ref):
    if case == EARLY:
        sum_ref[0:1, :] = jnp.zeros((1, WIDE), F32)
    for half in halves_of(case):
        a, b = rows_of(case, half)
        ln = lanes(half)
        dp = nt(v[a:b], g4[ln, :])
        dp_ref[a:b, ln] = dp
        sum_ref[0:1, ln] = jnp.sum(fold(p_ref[a:b, ln].astype(F32) * dp, jnp.add), axis=0, keepdims=True)


def joined(case, parts):
    blank = jnp.zeros((HALF, HEAD_DIM), F32)
    full = []
    for half, x in zip(halves_of(case), parts):
        a, b = rows_of(case, half)
        x = jnp.concatenate([blank, x], 0) if a else x
        full.append(jnp.concatenate([x, blank], 0) if b < TOK else x)
    return sum(full[1:], full[0])


def value_grad(case, g4, p_ref, factor):
    parts = []
    for half in halves_of(case):
        a, b = rows_of(case, half)
        ln = lanes(half)
        probs = p_ref[a:b, ln].astype(F32) * factor[:, ln]
        parts.append(nn(probs.astype(BF), g4[ln, :]))
    return joined(case, parts)


def key_query_grad(case, k, q4, p_ref, dp_ref, factor, delta):
    dk, dq = [], []
    for half in halves_of(case):
        a, b = rows_of(case, half)
        ln = lanes(half)
        probs = p_ref[a:b, ln].astype(F32) * factor[:, ln]
        ds = (probs * (dp_ref[a:b, ln] - delta[:, ln])).astype(BF)
        dk.append(nn(ds, q4[ln, :]) * SCALE)
        dq.append(nn(k[a:b].astype(F32).T.astype(BF), ds))
    return joined(case, dk), dq


def near(before_ref, distance):
    return before_ref[0] > (distance - 1) * TOK


def gated(distance, before_ref, work, other):
    if distance == 0:
        work()
    else:
        pl.when(near(before_ref, distance))(work)
        pl.when(jnp.logical_not(near(before_ref, distance)))(other)


def no_probs(stat_ref):
    stat_ref[0:1, :] = jnp.full((1, WIDE), NEG, F32)
    stat_ref[1:2, :] = jnp.zeros((1, WIDE), F32)


def probs_kernel(distance, before_ref, start_ref, q_ref, k_ref, *outs):
    i = pl.program_id(0)
    if distance == 0:
        q4_ref, p_ref, stat_ref = outs
        q4 = q4_ref.at[i]
        regroup(q4, q_ref)
    else:
        p_ref, stat_ref = outs
        q4 = q_ref.at[i]
    gated(
        distance,
        before_ref,
        lambda: local_probs(case_of(distance), distance, k_ref[...], q4, start_ref, p_ref.at[i], stat_ref.at[i]),
        lambda: no_probs(stat_ref.at[i]),
    )


def dprobs_kernel(distance, before_ref, g_ref, v_ref, p_ref, *outs):
    i = pl.program_id(0)
    if distance == 0:
        g4_ref, dp_ref, sum_ref = outs
        g4 = g4_ref.at[i]
        regroup(g4, g_ref)
    else:
        dp_ref, sum_ref = outs
        g4 = g_ref.at[i]

    def other():
        sum_ref[i, 0:1, :] = jnp.zeros((1, WIDE), F32)

    gated(
        distance,
        before_ref,
        lambda: local_dprobs(case_of(distance), v_ref[...], g4, p_ref.at[i], dp_ref.at[i], sum_ref.at[i]),
        other,
    )


def far_cases(before_ref, work):
    before = before_ref[0]
    edge = REACH * TOK - HALF
    pl.when(before > edge)(functools.partial(work, EARLY))
    pl.when((before > (REACH - 1) * TOK) & (before <= edge))(functools.partial(work, LATE))
    pl.when(before <= (REACH - 1) * TOK)(functools.partial(work, None))


def far_value_kernel(before_ref, start_ref, q4_ref, g4_ref, k_ref, s0, s1, s2, part_ref, p_ref, row_ref, stat_ref):
    def work(case):
        for n in range(FAR_GROUPS):
            i = pl.program_id(0) * FAR_GROUPS + n
            at = slice(n * HEAD_DIM, (n + 1) * HEAD_DIM)
            row, stat = row_ref.at[i], stat_ref.at[n]
            stats = [s0.at[i], s1.at[i], s2.at[i]]
            if case:
                local_probs(case, REACH, k_ref[:, at], q4_ref.at[i], start_ref, p_ref.at[i], stat)
                stats.append(stat)
            top = functools.reduce(jnp.maximum, [s[0:1, :] for s in stats])
            weight = [jnp.exp2((s[0:1, :] - top) * (SCALE * LOG2E)) for s in stats]
            total = sum(w * s[1:2, :] for w, s in zip(weight, stats))
            for d, w in enumerate(weight):
                row[d : d + 1, :] = w / total
            if case:
                factor = row[REACH : REACH + 1, :]
                part_ref[:, at] = value_grad(case, g4_ref.at[i], p_ref.at[i], factor).astype(BF)
            else:
                part_ref[:, at] = jnp.zeros((TOK, HEAD_DIM), BF)

    far_cases(before_ref, work)


def far_key_kernel(before_ref, q4_ref, g4_ref, k_ref, v_ref, p_ref, row_ref, e0, e1, e2, part_ref, dq_ref, delta_ref, dp_ref, sum_ref):
    def work(case):
        for n in range(FAR_GROUPS):
            i = pl.program_id(0) * FAR_GROUPS + n
            at = slice(n * HEAD_DIM, (n + 1) * HEAD_DIM)
            row, dq_out = row_ref.at[i], dq_ref.at[i]
            sums = [e0.at[i], e1.at[i], e2.at[i]]
            if case:
                local_dprobs(case, v_ref[:, at], g4_ref.at[i], p_ref.at[i], dp_ref.at[n], sum_ref.at[n])
                sums.append(sum_ref.at[n])
            delta = sum(row[d : d + 1, :] * s[0:1, :] for d, s in enumerate(sums))
            delta_ref[i, 0:1, :] = delta
            if not case:
                part_ref[:, at] = jnp.zeros((TOK, HEAD_DIM), BF)
                dq_out[...] = jnp.zeros_like(dq_out)
                continue
            factor = row[REACH : REACH + 1, :]
            dk, dq = key_query_grad(case, k_ref[:, at], q4_ref.at[i], p_ref.at[i], dp_ref.at[n], factor, delta)
            part_ref[:, at] = dk.astype(BF)
            if case == EARLY:
                dq_out[:, lanes(1)] = jnp.zeros((HEAD_DIM, LANES), F32)
            for half, x in zip(halves_of(case), dq):
                dq_out[:, lanes(half)] = x

    far_cases(before_ref, work)


def value_kernel(distance, before_ref, g4_ref, p_ref, row_ref, part_ref):
    i = pl.program_id(0)

    def work():
        factor = row_ref[i, distance : distance + 1, :]
        part_ref[...] = value_grad(case_of(distance), g4_ref.at[i], p_ref.at[i], factor).astype(part_ref.dtype)

    def other():
        part_ref[...] = jnp.zeros_like(part_ref)

    gated(distance, before_ref, work, other)


def key_kernel(distance, before_ref, q4_ref, k_ref, p_ref, dp_ref, row_ref, delta_ref, dq_in, part_ref, dq_ref):
    i = pl.program_id(0)
    dq_old = dq_in.at[i]

    def work():
        dk, dq = key_query_grad(
            case_of(distance),
            k_ref[...],
            q4_ref.at[i],
            p_ref.at[i],
            dp_ref.at[i],
            row_ref[i, distance : distance + 1, :],
            delta_ref[i, 0:1, :],
        )
        part_ref[...] = dk.astype(part_ref.dtype)
        for half in range(2):
            total = dq_old[:, lanes(half)] + dq[half]
            if distance:
                dq_ref[i, :, lanes(half)] = total
                continue
            total = total * SCALE
            for h in range(GROUP):
                dq_ref[half * HALF : (half + 1) * HALF, h * 128 : (h + 1) * 128] = (
                    total[:, h * HALF : (h + 1) * HALF].T.astype(BF)
                )

    def other():
        part_ref[...] = jnp.zeros_like(part_ref)
        dq_ref[i] = dq_old[...]

    gated(distance, before_ref, work, other)


SMEM = pl.BlockSpec(memory_space=pltpu.SMEM)
HELD = pl.BlockSpec(memory_space=pltpu.VMEM)
START = pl.BlockSpec((1, TOK), lambda i: (0, 0))
QUERY = pl.BlockSpec((TOK, GROUP * HEAD_DIM), lambda i: (0, i))
KEY = pl.BlockSpec((TOK, HEAD_DIM), lambda i: (0, i))


def held(rows, width, dtype):
    return HELD, pltpu.VMEM((KV_HEADS, rows, width), dtype)


GROUPED = held(WIDE, HEAD_DIM, BF)
PROBS = held(TOK, WIDE, BF)
DPROBS = held(TOK, WIDE, F32)
STATS = held(8, WIDE, F32)
QUERY_GRAD = held(HEAD_DIM, WIDE, F32)
FAR_KEY = pl.BlockSpec((TOK, FAR_GROUPS * HEAD_DIM), lambda i: (0, i))
PART = KEY, jax.ShapeDtypeStruct((TOK, KV_HEADS * HEAD_DIM), BF)
FAR_PART = FAR_KEY, PART[1]
OWN = KEY, jax.ShapeDtypeStruct((TOK, KV_HEADS * HEAD_DIM), F32)
QUERY_OUT = QUERY, jax.ShapeDtypeStruct((TOK, KV_HEADS * GROUP * HEAD_DIM), BF)


def call(kernel, in_specs, outs, matmuls, args, scratch=(), steps=KV_HEADS):
    return pl.pallas_call(
        kernel,
        grid=(steps,),
        in_specs=in_specs,
        out_specs=[spec for spec, _ in outs],
        out_shape=[shape for _, shape in outs],
        scratch_shapes=scratch,
        compiler_params=pltpu.CompilerParams(vmem_limit_bytes=VMEM_LIMIT),
        cost_estimate=pl.CostEstimate(
            flops=matmuls * KV_HEADS * 2 * TOK * WIDE * HEAD_DIM, bytes_accessed=2**20, transcendentals=0
        ),
    )(*args)


def probs_of(distance, before, start, q, k):
    own = distance == 0
    return call(
        functools.partial(probs_kernel, distance),
        [SMEM, START, QUERY if own else HELD, KEY],
        [GROUPED] * own + [PROBS, STATS],
        1,
        (before, start, q, k),
    )


def dprobs_of(distance, before, g, v, p):
    own = distance == 0
    return call(
        functools.partial(dprobs_kernel, distance),
        [SMEM, QUERY if own else HELD, KEY, HELD],
        [GROUPED] * own + [DPROBS, STATS],
        1,
        (before, g, v, p),
    )


def far_value(before, start, q4, g4, k, *stats):
    return call(
        far_value_kernel,
        [SMEM, START, HELD, HELD, FAR_KEY, HELD, HELD, HELD],
        [FAR_PART, PROBS, STATS],
        2,
        (before, start, q4, g4, k, *stats),
        [pltpu.VMEM((FAR_GROUPS, 8, WIDE), F32)],
        KV_HEADS // FAR_GROUPS,
    )


def far_key(before, q4, g4, k, v, p, row, *sums):
    return call(
        far_key_kernel,
        [SMEM, HELD, HELD, FAR_KEY, FAR_KEY] + [HELD] * 5,
        [FAR_PART, QUERY_GRAD, STATS],
        3,
        (before, q4, g4, k, v, p, row, *sums),
        [pltpu.VMEM((FAR_GROUPS, TOK, WIDE), F32), pltpu.VMEM((FAR_GROUPS, 8, WIDE), F32)],
        KV_HEADS // FAR_GROUPS,
    )


def value_part(distance, before, g4, p, row):
    return call(
        functools.partial(value_kernel, distance),
        [SMEM, HELD, HELD, HELD],
        [PART if distance else OWN],
        1,
        (before, g4, p, row),
    )[0]


def key_part(distance, before, q4, k, p, dp, row, delta, dq):
    return call(
        functools.partial(key_kernel, distance),
        [SMEM, HELD, KEY] + [HELD] * 5,
        [PART, QUERY_GRAD] if distance else [OWN, QUERY_OUT],
        2,
        (before, q4, k, p, dp, row, delta, dq),
    )


def shift(x, distance):
    devices = range(lax.axis_size(("dp", "ctx")))
    route = [(i - distance, i) for i in devices if i - distance in devices]
    return lax.ppermute(x, ("dp", "ctx"), route)


def add(a, b):
    return (a.astype(F32) + b.astype(F32)).astype(BF)


def after(x, *others):
    return lax.optimization_barrier((x, *others))[0]


def in_hbm(x):
    return pltpu.with_memory_space_constraint(x, pltpu.HBM)


def on_device(queries, keys, values, grad_out, doc_lengths):
    first = lax.axis_index(("dp", "ctx")) * TOK
    ends = jnp.cumsum(doc_lengths)
    pos = first + jnp.arange(TOK, dtype=jnp.int32)
    start = jnp.max(jnp.where(ends[:, None] <= pos[None, :], ends[:, None], 0), axis=0) - first
    before = jnp.maximum(-start[:1], 0)
    start = start[None]
    k, v = [keys], [values]
    k.append(shift(k[0], 1))
    v.append(shift(after(values, start), 1))
    q4, p0, stat0 = probs_of(0, before, start, in_hbm(queries), in_hbm(keys))
    p, dp, stat, total = [p0], [], [stat0], []
    done = stat0
    for d in (1, 2):
        k[d] = after(k[d], done)
        k.append(shift(k[d], 1))
        x, y = probs_of(d, before, start, q4, k[d])
        p.append(x)
        stat.append(y)
        v[d] = after(v[d], y)
        v.append(shift(v[d], 1))
        if d == 1:
            late = after(grad_out, v[d])
            g4, dp0, sum0 = dprobs_of(0, before, in_hbm(late), in_hbm(values), p0)
            dp.append(dp0)
            total.append(sum0)
        x, y = dprobs_of(d, before, g4, v[d], p[d])
        dp.append(x)
        total.append(y)
        done = y
    k[3] = after(k[3], done)
    part, p3, row = far_value(before, start, q4, g4, k[3], *stat)
    gv = shift(part, -1)
    v[3] = after(v[3], part)
    part, dq, delta = far_key(before, q4, g4, k[3], v[3], p3, row, *total)
    gk = shift(part, -1)
    done = part
    for d in (2, 1):
        part = value_part(d, before, g4, p[d], after(row, done))
        gv = add(after(gv, part), part)
        done = gv
        gv = shift(gv, -1)
        part, dq = key_part(d, before, q4, k[d], p[d], dp[d], after(row, done), delta, dq)
        gk = add(after(gk, part), part)
        done = gk
        gk = shift(gk, -1)
    own_v = value_part(0, before, g4, p0, after(row, done))
    own_k, grad_queries = key_part(0, before, q4, keys, p0, dp0, after(row, own_v), delta, dq)
    gv = after(gv, own_k)
    return grad_queries, add(own_k, gk), add(own_v, gv)


def solution(mesh):
    spec = P(("dp", "ctx"), None)
    return jax.shard_map(
        on_device,
        mesh=mesh,
        in_specs=(spec, spec, spec, spec, P()),
        out_specs=(spec, spec, spec),
        check_vma=False,
    )
```

```python
import functools

import jax
import jax.numpy as jnp
from jax import lax
from jax.experimental import pallas as pl
from jax.experimental.pallas import tpu as pltpu
from jax.sharding import PartitionSpec as P

HEAD_DIM = 128
REACH = 3
TOK = 256
HALF = 128
GROUP = 4
KV_HEADS = 4
FAR_GROUPS = 4
LANES = GROUP * HALF
WIDE = 2 * LANES
SCALE = HEAD_DIM**-0.5
LOG2E = 1.4426950408889634
NEG = -1e30
F32 = jnp.float32
BF = jnp.bfloat16
VMEM_LIMIT = 20 * 2**20


def nt(a, b):
    return lax.dot_general(a, b, (((1,), (1,)), ((), ())), preferred_element_type=F32)


def nn(a, b):
    return lax.dot_general(a, b, (((1,), (0,)), ((), ())), preferred_element_type=F32)


def fold(x, op):
    total = x[:8]
    for i in range(1, x.shape[0] // 8):
        total = op(total, x[i * 8 : (i + 1) * 8])
    return total


def lanes(half):
    return slice(half * LANES, (half + 1) * LANES)


OWN_BLOCK, NEAR_BLOCK, LATE, EARLY = "own", "near", "late", "early"


def rows_of(case, half):
    if case == OWN_BLOCK and half == 0:
        return 0, HALF
    if case == LATE:
        return HALF, TOK
    if case == EARLY and half == 1:
        return 0, 0
    return 0, TOK


def halves_of(case):
    return [half for half in range(2) if rows_of(case, half)[1]]


def case_of(distance):
    return NEAR_BLOCK if distance else OWN_BLOCK


def regroup(dst, src):
    for half in range(2):
        for h in range(GROUP):
            at = half * LANES + h * HALF
            dst[at : at + HALF, :] = src[half * HALF : (half + 1) * HALF, h * 128 : (h + 1) * 128]


def masked_scores(case, distance, half, k, q4, start_ref):
    a, b = rows_of(case, half)
    s = nt(k[a:b], q4[lanes(half), :])
    start = start_ref[:, half * HALF : (half + 1) * HALF]
    at = lax.broadcasted_iota(jnp.int32, (b - a, HALF), 0) + (a - distance * TOK)
    ok = at >= start
    if case == OWN_BLOCK:
        ok = ok & (at <= lax.broadcasted_iota(jnp.int32, (b - a, HALF), 1) + half * HALF)
    return jnp.concatenate(
        [jnp.where(ok, s[:, h * HALF : (h + 1) * HALF], NEG) for h in range(GROUP)], axis=1
    )


def local_probs(case, distance, k, q4, start_ref, p_ref, stat_ref):
    if case == EARLY:
        no_probs(stat_ref)
    for half in halves_of(case):
        a, b = rows_of(case, half)
        ln = lanes(half)
        s = masked_scores(case, distance, half, k, q4, start_ref)
        top = jnp.max(fold(s, jnp.maximum), axis=0, keepdims=True)
        p = jnp.exp2((s - top) * (SCALE * LOG2E))
        p_ref[a:b, ln] = p.astype(BF)
        stat_ref[0:1, ln] = top
        stat_ref[1:2, ln] = jnp.sum(fold(p, jnp.add), axis=0, keepdims=True)


def local_dprobs(case, v, g4, p_ref, dp_ref, sum_ref):
    if case == EARLY:
        sum_ref[0:1, :] = jnp.zeros((1, WIDE), F32)
    for half in halves_of(case):
        a, b = rows_of(case, half)
        ln = lanes(half)
        dp = nt(v[a:b], g4[ln, :])
        dp_ref[a:b, ln] = dp
        sum_ref[0:1, ln] = jnp.sum(fold(p_ref[a:b, ln].astype(F32) * dp, jnp.add), axis=0, keepdims=True)


def joined(case, parts):
    blank = jnp.zeros((HALF, HEAD_DIM), F32)
    full = []
    for half, x in zip(halves_of(case), parts):
        a, b = rows_of(case, half)
        x = jnp.concatenate([blank, x], 0) if a else x
        full.append(jnp.concatenate([x, blank], 0) if b < TOK else x)
    return sum(full[1:], full[0])


def value_grad(case, g4, p_ref, factor):
    parts = []
    for half in halves_of(case):
        a, b = rows_of(case, half)
        ln = lanes(half)
        probs = p_ref[a:b, ln].astype(F32) * factor[:, ln]
        parts.append(nn(probs.astype(BF), g4[ln, :]))
    return joined(case, parts)


def key_query_grad(case, k, q4, p_ref, dp_ref, factor, delta):
    dk, dq = [], []
    for half in halves_of(case):
        a, b = rows_of(case, half)
        ln = lanes(half)
        probs = p_ref[a:b, ln].astype(F32) * factor[:, ln]
        ds = (probs * (dp_ref[a:b, ln] - delta[:, ln])).astype(BF)
        dk.append(nn(ds, q4[ln, :]) * SCALE)
        dq.append(nn(k[a:b].astype(F32).T.astype(BF), ds))
    return joined(case, dk), dq


def near(before_ref, distance):
    return before_ref[0] > (distance - 1) * TOK


def gated(distance, before_ref, work, other):
    if distance == 0:
        work()
    else:
        pl.when(near(before_ref, distance))(work)
        pl.when(jnp.logical_not(near(before_ref, distance)))(other)


def no_probs(stat_ref):
    stat_ref[0:1, :] = jnp.full((1, WIDE), NEG, F32)
    stat_ref[1:2, :] = jnp.zeros((1, WIDE), F32)


def probs_kernel(distance, before_ref, start_ref, q_ref, k_ref, *outs):
    i = pl.program_id(0)
    if distance == 0:
        q4_ref, p_ref, stat_ref = outs
        q4 = q4_ref.at[i]
        regroup(q4, q_ref)
    else:
        p_ref, stat_ref = outs
        q4 = q_ref.at[i]
    gated(
        distance,
        before_ref,
        lambda: local_probs(case_of(distance), distance, k_ref[...], q4, start_ref, p_ref.at[i], stat_ref.at[i]),
        lambda: no_probs(stat_ref.at[i]),
    )


def dprobs_kernel(distance, before_ref, g_ref, v_ref, p_ref, *outs):
    i = pl.program_id(0)
    if distance == 0:
        g4_ref, dp_ref, sum_ref = outs
        g4 = g4_ref.at[i]
        regroup(g4, g_ref)
    else:
        dp_ref, sum_ref = outs
        g4 = g_ref.at[i]

    def other():
        sum_ref[i, 0:1, :] = jnp.zeros((1, WIDE), F32)

    gated(
        distance,
        before_ref,
        lambda: local_dprobs(case_of(distance), v_ref[...], g4, p_ref.at[i], dp_ref.at[i], sum_ref.at[i]),
        other,
    )


def far_cases(before_ref, work):
    before = before_ref[0]
    edge = REACH * TOK - HALF
    pl.when(before > edge)(functools.partial(work, EARLY))
    pl.when((before > (REACH - 1) * TOK) & (before <= edge))(functools.partial(work, LATE))
    pl.when(before <= (REACH - 1) * TOK)(functools.partial(work, None))


def far_value_kernel(before_ref, start_ref, q4_ref, g4_ref, k_ref, s0, s1, s2, part_ref, p_ref, row_ref, stat_ref):
    def work(case):
        for n in range(FAR_GROUPS):
            i = pl.program_id(0) * FAR_GROUPS + n
            at = slice(n * HEAD_DIM, (n + 1) * HEAD_DIM)
            row, stat = row_ref.at[i], stat_ref.at[n]
            stats = [s0.at[i], s1.at[i], s2.at[i]]
            if case:
                local_probs(case, REACH, k_ref[:, at], q4_ref.at[i], start_ref, p_ref.at[i], stat)
                stats.append(stat)
            top = functools.reduce(jnp.maximum, [s[0:1, :] for s in stats])
            weight = [jnp.exp2((s[0:1, :] - top) * (SCALE * LOG2E)) for s in stats]
            total = sum(w * s[1:2, :] for w, s in zip(weight, stats))
            for d, w in enumerate(weight):
                row[d : d + 1, :] = w / total
            if case:
                factor = row[REACH : REACH + 1, :]
                part_ref[:, at] = value_grad(case, g4_ref.at[i], p_ref.at[i], factor).astype(BF)
            else:
                part_ref[:, at] = jnp.zeros((TOK, HEAD_DIM), BF)

    far_cases(before_ref, work)


def far_key_kernel(before_ref, q4_ref, g4_ref, k_ref, v_ref, p_ref, row_ref, e0, e1, e2, part_ref, dq_ref, delta_ref, dp_ref, sum_ref):
    def work(case):
        for n in range(FAR_GROUPS):
            i = pl.program_id(0) * FAR_GROUPS + n
            at = slice(n * HEAD_DIM, (n + 1) * HEAD_DIM)
            row, dq_out = row_ref.at[i], dq_ref.at[i]
            sums = [e0.at[i], e1.at[i], e2.at[i]]
            if case:
                local_dprobs(case, v_ref[:, at], g4_ref.at[i], p_ref.at[i], dp_ref.at[n], sum_ref.at[n])
                sums.append(sum_ref.at[n])
            delta = sum(row[d : d + 1, :] * s[0:1, :] for d, s in enumerate(sums))
            delta_ref[i, 0:1, :] = delta
            if not case:
                part_ref[:, at] = jnp.zeros((TOK, HEAD_DIM), BF)
                dq_out[...] = jnp.zeros_like(dq_out)
                continue
            factor = row[REACH : REACH + 1, :]
            dk, dq = key_query_grad(case, k_ref[:, at], q4_ref.at[i], p_ref.at[i], dp_ref.at[n], factor, delta)
            part_ref[:, at] = dk.astype(BF)
            if case == EARLY:
                dq_out[:, lanes(1)] = jnp.zeros((HEAD_DIM, LANES), F32)
            for half, x in zip(halves_of(case), dq):
                dq_out[:, lanes(half)] = x

    far_cases(before_ref, work)


def value_kernel(distance, before_ref, g4_ref, p_ref, row_ref, part_ref):
    i = pl.program_id(0)

    def work():
        factor = row_ref[i, distance : distance + 1, :]
        part_ref[...] = value_grad(case_of(distance), g4_ref.at[i], p_ref.at[i], factor).astype(part_ref.dtype)

    def other():
        part_ref[...] = jnp.zeros_like(part_ref)

    gated(distance, before_ref, work, other)


def key_kernel(distance, before_ref, q4_ref, k_ref, p_ref, dp_ref, row_ref, delta_ref, dq_in, part_ref, dq_ref):
    i = pl.program_id(0)
    dq_old = dq_in.at[i]

    def work():
        dk, dq = key_query_grad(
            case_of(distance),
            k_ref[...],
            q4_ref.at[i],
            p_ref.at[i],
            dp_ref.at[i],
            row_ref[i, distance : distance + 1, :],
            delta_ref[i, 0:1, :],
        )
        part_ref[...] = dk.astype(part_ref.dtype)
        for half in range(2):
            total = dq_old[:, lanes(half)] + dq[half]
            if distance:
                dq_ref[i, :, lanes(half)] = total
                continue
            total = total * SCALE
            for h in range(GROUP):
                dq_ref[half * HALF : (half + 1) * HALF, h * 128 : (h + 1) * 128] = (
                    total[:, h * HALF : (h + 1) * HALF].T.astype(BF)
                )

    def other():
        part_ref[...] = jnp.zeros_like(part_ref)
        dq_ref[i] = dq_old[...]

    gated(distance, before_ref, work, other)


SMEM = pl.BlockSpec(memory_space=pltpu.SMEM)
HELD = pl.BlockSpec(memory_space=pltpu.VMEM)
START = pl.BlockSpec((1, TOK), lambda i: (0, 0))
QUERY = pl.BlockSpec((TOK, GROUP * HEAD_DIM), lambda i: (0, i))
KEY = pl.BlockSpec((TOK, HEAD_DIM), lambda i: (0, i))


def held(rows, width, dtype):
    return HELD, pltpu.VMEM((KV_HEADS, rows, width), dtype)


GROUPED = held(WIDE, HEAD_DIM, BF)
PROBS = held(TOK, WIDE, BF)
DPROBS = held(TOK, WIDE, F32)
STATS = held(8, WIDE, F32)
QUERY_GRAD = held(HEAD_DIM, WIDE, F32)
FAR_KEY = pl.BlockSpec((TOK, FAR_GROUPS * HEAD_DIM), lambda i: (0, i))
PART = KEY, jax.ShapeDtypeStruct((TOK, KV_HEADS * HEAD_DIM), BF)
FAR_PART = FAR_KEY, PART[1]
OWN = KEY, jax.ShapeDtypeStruct((TOK, KV_HEADS * HEAD_DIM), F32)
QUERY_OUT = QUERY, jax.ShapeDtypeStruct((TOK, KV_HEADS * GROUP * HEAD_DIM), BF)


def call(kernel, in_specs, outs, matmuls, args, scratch=(), steps=KV_HEADS):
    return pl.pallas_call(
        kernel,
        grid=(steps,),
        in_specs=in_specs,
        out_specs=[spec for spec, _ in outs],
        out_shape=[shape for _, shape in outs],
        scratch_shapes=scratch,
        compiler_params=pltpu.CompilerParams(vmem_limit_bytes=VMEM_LIMIT),
        cost_estimate=pl.CostEstimate(
            flops=matmuls * KV_HEADS * 2 * TOK * WIDE * HEAD_DIM, bytes_accessed=2**20, transcendentals=0
        ),
    )(*args)


def probs_of(distance, before, start, q, k):
    own = distance == 0
    return call(
        functools.partial(probs_kernel, distance),
        [SMEM, START, QUERY if own else HELD, KEY],
        [GROUPED] * own + [PROBS, STATS],
        1,
        (before, start, q, k),
    )


def dprobs_of(distance, before, g, v, p):
    own = distance == 0
    return call(
        functools.partial(dprobs_kernel, distance),
        [SMEM, QUERY if own else HELD, KEY, HELD],
        [GROUPED] * own + [DPROBS, STATS],
        1,
        (before, g, v, p),
    )


def far_value(before, start, q4, g4, k, *stats):
    return call(
        far_value_kernel,
        [SMEM, START, HELD, HELD, FAR_KEY, HELD, HELD, HELD],
        [FAR_PART, PROBS, STATS],
        2,
        (before, start, q4, g4, k, *stats),
        [pltpu.VMEM((FAR_GROUPS, 8, WIDE), F32)],
        KV_HEADS // FAR_GROUPS,
    )


def far_key(before, q4, g4, k, v, p, row, *sums):
    return call(
        far_key_kernel,
        [SMEM, HELD, HELD, FAR_KEY, FAR_KEY] + [HELD] * 5,
        [FAR_PART, QUERY_GRAD, STATS],
        3,
        (before, q4, g4, k, v, p, row, *sums),
        [pltpu.VMEM((FAR_GROUPS, TOK, WIDE), F32), pltpu.VMEM((FAR_GROUPS, 8, WIDE), F32)],
        KV_HEADS // FAR_GROUPS,
    )


def value_part(distance, before, g4, p, row):
    return call(
        functools.partial(value_kernel, distance),
        [SMEM, HELD, HELD, HELD],
        [PART if distance else OWN],
        1,
        (before, g4, p, row),
    )[0]


def key_part(distance, before, q4, k, p, dp, row, delta, dq):
    return call(
        functools.partial(key_kernel, distance),
        [SMEM, HELD, KEY] + [HELD] * 5,
        [PART, QUERY_GRAD] if distance else [OWN, QUERY_OUT],
        2,
        (before, q4, k, p, dp, row, delta, dq),
    )


def shift(x, distance):
    devices = range(lax.axis_size(("dp", "ctx")))
    route = [(i - distance, i) for i in devices if i - distance in devices]
    return lax.ppermute(x, ("dp", "ctx"), route)


def add(a, b):
    return (a.astype(F32) + b.astype(F32)).astype(BF)


def after(x, *others):
    return lax.optimization_barrier((x, *others))[0]


def in_hbm(x):
    return pltpu.with_memory_space_constraint(x, pltpu.HBM)


def on_device(queries, keys, values, grad_out, doc_lengths):
    first = lax.axis_index(("dp", "ctx")) * TOK
    ends = jnp.cumsum(doc_lengths)
    pos = first + jnp.arange(TOK, dtype=jnp.int32)
    start = jnp.max(jnp.where(ends[:, None] <= pos[None, :], ends[:, None], 0), axis=0) - first
    before = jnp.maximum(-start[:1], 0)
    start = start[None]
    k, v = [keys], [values]
    k.append(shift(k[0], 1))
    v.append(shift(after(values, start), 1))
    q4, p0, stat0 = probs_of(0, before, start, in_hbm(queries), in_hbm(keys))
    p, dp, stat, total = [p0], [], [stat0], []
    done = stat0
    for d in (1, 2):
        k[d] = after(k[d], done)
        k.append(shift(k[d], 1))
        x, y = probs_of(d, before, start, q4, k[d])
        p.append(x)
        stat.append(y)
        v[d] = after(v[d], y)
        v.append(shift(v[d], 1))
        if d == 1:
            late = after(grad_out, v[d])
            g4, dp0, sum0 = dprobs_of(0, before, in_hbm(late), in_hbm(values), p0)
            dp.append(dp0)
            total.append(sum0)
        x, y = dprobs_of(d, before, g4, v[d], p[d])
        dp.append(x)
        total.append(y)
        done = y
    k[3] = after(k[3], done)
    part, p3, row = far_value(before, start, q4, g4, k[3], *stat)
    gv = shift(part, -1)
    v[3] = after(v[3], part)
    part, dq, delta = far_key(before, q4, g4, k[3], v[3], p3, row, *total)
    gk = shift(part, -1)
    done = part
    for d in (2, 1):
        part = value_part(d, before, g4, p[d], after(row, done))
        gv = add(after(gv, part), part)
        done = gv
        gv = shift(gv, -1)
        part, dq = key_part(d, before, q4, k[d], p[d], dp[d], after(row, done), delta, dq)
        gk = add(after(gk, part), part)
        done = gk
        gk = shift(gk, -1)
    own_v = value_part(0, before, g4, p0, after(row, done))
    own_k, grad_queries = key_part(0, before, q4, keys, p0, dp0, after(row, own_v), delta, dq)
    gv = after(gv, own_k)
    return grad_queries, add(own_k, gk), add(own_v, gv)


def solution(mesh):
    spec = P(("dp", "ctx"), None)
    return jax.shard_map(
        on_device,
        mesh=mesh,
        in_specs=(spec, spec, spec, spec, P()),
        out_specs=(spec, spec, spec),
        check_vma=False,
    )
```

```python
import functools

import jax
import jax.numpy as jnp
from jax import lax
from jax.experimental import pallas as pl
from jax.experimental.pallas import tpu as pltpu
from jax.sharding import PartitionSpec as P

HEAD_DIM = 128
REACH = 3
TOK = 256
HALF = 128
GROUP = 4
KV_HEADS = 4
FAR_GROUPS = 4
LANES = GROUP * HALF
WIDE = 2 * LANES
SCALE = HEAD_DIM**-0.5
LOG2E = 1.4426950408889634
NEG = -1e30
F32 = jnp.float32
BF = jnp.bfloat16
VMEM_LIMIT = 20 * 2**20


def nt(a, b):
    return lax.dot_general(a, b, (((1,), (1,)), ((), ())), preferred_element_type=F32)


def nn(a, b):
    return lax.dot_general(a, b, (((1,), (0,)), ((), ())), preferred_element_type=F32)


def fold(x, op):
    total = x[:8]
    for i in range(1, x.shape[0] // 8):
        total = op(total, x[i * 8 : (i + 1) * 8])
    return total


def lanes(half):
    return slice(half * LANES, (half + 1) * LANES)


OWN_BLOCK, NEAR_BLOCK, LATE, EARLY = "own", "near", "late", "early"


def rows_of(case, half):
    if case == OWN_BLOCK and half == 0:
        return 0, HALF
    if case == LATE:
        return HALF, TOK
    if case == EARLY and half == 1:
        return 0, 0
    return 0, TOK


def halves_of(case):
    return [half for half in range(2) if rows_of(case, half)[1]]


def case_of(distance):
    return NEAR_BLOCK if distance else OWN_BLOCK


def regroup(dst, src):
    for half in range(2):
        for h in range(GROUP):
            at = half * LANES + h * HALF
            dst[at : at + HALF, :] = src[half * HALF : (half + 1) * HALF, h * 128 : (h + 1) * 128]


def masked_scores(case, distance, half, k, q4, start_ref):
    a, b = rows_of(case, half)
    s = nt(k[a:b], q4[lanes(half), :])
    start = start_ref[:, half * HALF : (half + 1) * HALF]
    at = lax.broadcasted_iota(jnp.int32, (b - a, HALF), 0) + (a - distance * TOK)
    ok = at >= start
    if case == OWN_BLOCK:
        ok = ok & (at <= lax.broadcasted_iota(jnp.int32, (b - a, HALF), 1) + half * HALF)
    return jnp.concatenate(
        [jnp.where(ok, s[:, h * HALF : (h + 1) * HALF], NEG) for h in range(GROUP)], axis=1
    )


def local_probs(case, distance, k, q4, start_ref, p_ref, stat_ref):
    if case == EARLY:
        no_probs(stat_ref)
    for half in halves_of(case):
        a, b = rows_of(case, half)
        ln = lanes(half)
        s = masked_scores(case, distance, half, k, q4, start_ref)
        top = jnp.max(fold(s, jnp.maximum), axis=0, keepdims=True)
        p = jnp.exp2((s - top) * (SCALE * LOG2E))
        p_ref[a:b, ln] = p.astype(BF)
        stat_ref[0:1, ln] = top
        stat_ref[1:2, ln] = jnp.sum(fold(p, jnp.add), axis=0, keepdims=True)


def local_dprobs(case, v, g4, p_ref, dp_ref, sum_ref):
    if case == EARLY:
        sum_ref[0:1, :] = jnp.zeros((1, WIDE), F32)
    for half in halves_of(case):
        a, b = rows_of(case, half)
        ln = lanes(half)
        dp = nt(v[a:b], g4[ln, :])
        dp_ref[a:b, ln] = dp
        sum_ref[0:1, ln] = jnp.sum(fold(p_ref[a:b, ln].astype(F32) * dp, jnp.add), axis=0, keepdims=True)


def joined(case, parts):
    blank = jnp.zeros((HALF, HEAD_DIM), F32)
    full = []
    for half, x in zip(halves_of(case), parts):
        a, b = rows_of(case, half)
        x = jnp.concatenate([blank, x], 0) if a else x
        full.append(jnp.concatenate([x, blank], 0) if b < TOK else x)
    return sum(full[1:], full[0])


def value_grad(case, g4, p_ref, factor):
    parts = []
    for half in halves_of(case):
        a, b = rows_of(case, half)
        ln = lanes(half)
        probs = p_ref[a:b, ln].astype(F32) * factor[:, ln]
        parts.append(nn(probs.astype(BF), g4[ln, :]))
    return joined(case, parts)


def key_query_grad(case, k, q4, p_ref, dp_ref, factor, delta):
    dk, dq = [], []
    for half in halves_of(case):
        a, b = rows_of(case, half)
        ln = lanes(half)
        probs = p_ref[a:b, ln].astype(F32) * factor[:, ln]
        ds = (probs * (dp_ref[a:b, ln] - delta[:, ln])).astype(BF)
        dk.append(nn(ds, q4[ln, :]) * SCALE)
        dq.append(nn(k[a:b].astype(F32).T.astype(BF), ds))
    return joined(case, dk), dq


def near(before_ref, distance):
    return before_ref[0] > (distance - 1) * TOK


def gated(distance, before_ref, work, other):
    if distance == 0:
        work()
    else:
        pl.when(near(before_ref, distance))(work)
        pl.when(jnp.logical_not(near(before_ref, distance)))(other)


def no_probs(stat_ref):
    stat_ref[0:1, :] = jnp.full((1, WIDE), NEG, F32)
    stat_ref[1:2, :] = jnp.zeros((1, WIDE), F32)


def probs_kernel(distance, before_ref, start_ref, q_ref, k_ref, *outs):
    i = pl.program_id(0)
    if distance == 0:
        q4_ref, p_ref, stat_ref = outs
        q4 = q4_ref.at[i]
        regroup(q4, q_ref)
    else:
        p_ref, stat_ref = outs
        q4 = q_ref.at[i]
    gated(
        distance,
        before_ref,
        lambda: local_probs(case_of(distance), distance, k_ref[...], q4, start_ref, p_ref.at[i], stat_ref.at[i]),
        lambda: no_probs(stat_ref.at[i]),
    )


def dprobs_kernel(distance, before_ref, g_ref, v_ref, p_ref, *outs):
    i = pl.program_id(0)
    if distance == 0:
        g4_ref, dp_ref, sum_ref = outs
        g4 = g4_ref.at[i]
        regroup(g4, g_ref)
    else:
        dp_ref, sum_ref = outs
        g4 = g_ref.at[i]

    def other():
        sum_ref[i, 0:1, :] = jnp.zeros((1, WIDE), F32)

    gated(
        distance,
        before_ref,
        lambda: local_dprobs(case_of(distance), v_ref[...], g4, p_ref.at[i], dp_ref.at[i], sum_ref.at[i]),
        other,
    )


def far_cases(before_ref, work):
    before = before_ref[0]
    edge = REACH * TOK - HALF
    pl.when(before > edge)(functools.partial(work, EARLY))
    pl.when((before > (REACH - 1) * TOK) & (before <= edge))(functools.partial(work, LATE))
    pl.when(before <= (REACH - 1) * TOK)(functools.partial(work, None))


def far_value_kernel(before_ref, start_ref, q4_ref, g4_ref, k_ref, s0, s1, s2, part_ref, p_ref, row_ref, stat_ref):
    def work(case):
        for n in range(FAR_GROUPS):
            i = pl.program_id(0) * FAR_GROUPS + n
            at = slice(n * HEAD_DIM, (n + 1) * HEAD_DIM)
            row, stat = row_ref.at[i], stat_ref.at[n]
            stats = [s0.at[i], s1.at[i], s2.at[i]]
            if case:
                local_probs(case, REACH, k_ref[:, at], q4_ref.at[i], start_ref, p_ref.at[i], stat)
                stats.append(stat)
            top = functools.reduce(jnp.maximum, [s[0:1, :] for s in stats])
            weight = [jnp.exp2((s[0:1, :] - top) * (SCALE * LOG2E)) for s in stats]
            total = sum(w * s[1:2, :] for w, s in zip(weight, stats))
            for d, w in enumerate(weight):
                row[d : d + 1, :] = w / total
            if case:
                factor = row[REACH : REACH + 1, :]
                part_ref[:, at] = value_grad(case, g4_ref.at[i], p_ref.at[i], factor).astype(BF)
            else:
                part_ref[:, at] = jnp.zeros((TOK, HEAD_DIM), BF)

    far_cases(before_ref, work)


def far_key_kernel(before_ref, q4_ref, g4_ref, k_ref, v_ref, p_ref, row_ref, e0, e1, e2, part_ref, dq_ref, delta_ref, dp_ref, sum_ref):
    def work(case):
        for n in range(FAR_GROUPS):
            i = pl.program_id(0) * FAR_GROUPS + n
            at = slice(n * HEAD_DIM, (n + 1) * HEAD_DIM)
            row, dq_out = row_ref.at[i], dq_ref.at[i]
            sums = [e0.at[i], e1.at[i], e2.at[i]]
            if case:
                local_dprobs(case, v_ref[:, at], g4_ref.at[i], p_ref.at[i], dp_ref.at[n], sum_ref.at[n])
                sums.append(sum_ref.at[n])
            delta = sum(row[d : d + 1, :] * s[0:1, :] for d, s in enumerate(sums))
            delta_ref[i, 0:1, :] = delta
            if not case:
                part_ref[:, at] = jnp.zeros((TOK, HEAD_DIM), BF)
                dq_out[...] = jnp.zeros_like(dq_out)
                continue
            factor = row[REACH : REACH + 1, :]
            dk, dq = key_query_grad(case, k_ref[:, at], q4_ref.at[i], p_ref.at[i], dp_ref.at[n], factor, delta)
            part_ref[:, at] = dk.astype(BF)
            if case == EARLY:
                dq_out[:, lanes(1)] = jnp.zeros((HEAD_DIM, LANES), F32)
            for half, x in zip(halves_of(case), dq):
                dq_out[:, lanes(half)] = x

    far_cases(before_ref, work)


def value_kernel(distance, before_ref, g4_ref, p_ref, row_ref, part_ref):
    i = pl.program_id(0)

    def work():
        factor = row_ref[i, distance : distance + 1, :]
        part_ref[...] = value_grad(case_of(distance), g4_ref.at[i], p_ref.at[i], factor).astype(part_ref.dtype)

    def other():
        part_ref[...] = jnp.zeros_like(part_ref)

    gated(distance, before_ref, work, other)


def key_kernel(distance, before_ref, q4_ref, k_ref, p_ref, dp_ref, row_ref, delta_ref, dq_in, part_ref, dq_ref):
    i = pl.program_id(0)
    dq_old = dq_in.at[i]

    def work():
        dk, dq = key_query_grad(
            case_of(distance),
            k_ref[...],
            q4_ref.at[i],
            p_ref.at[i],
            dp_ref.at[i],
            row_ref[i, distance : distance + 1, :],
            delta_ref[i, 0:1, :],
        )
        part_ref[...] = dk.astype(part_ref.dtype)
        for half in range(2):
            total = dq_old[:, lanes(half)] + dq[half]
            if distance:
                dq_ref[i, :, lanes(half)] = total
                continue
            total = total * SCALE
            for h in range(GROUP):
                dq_ref[half * HALF : (half + 1) * HALF, h * 128 : (h + 1) * 128] = (
                    total[:, h * HALF : (h + 1) * HALF].T.astype(BF)
                )

    def other():
        part_ref[...] = jnp.zeros_like(part_ref)
        dq_ref[i] = dq_old[...]

    gated(distance, before_ref, work, other)


SMEM = pl.BlockSpec(memory_space=pltpu.SMEM)
HELD = pl.BlockSpec(memory_space=pltpu.VMEM)
START = pl.BlockSpec((1, TOK), lambda i: (0, 0))
QUERY = pl.BlockSpec((TOK, GROUP * HEAD_DIM), lambda i: (0, i))
KEY = pl.BlockSpec((TOK, HEAD_DIM), lambda i: (0, i))


def held(rows, width, dtype):
    return HELD, pltpu.VMEM((KV_HEADS, rows, width), dtype)


GROUPED = held(WIDE, HEAD_DIM, BF)
PROBS = held(TOK, WIDE, BF)
DPROBS = held(TOK, WIDE, F32)
STATS = held(8, WIDE, F32)
QUERY_GRAD = held(HEAD_DIM, WIDE, F32)
FAR_KEY = pl.BlockSpec((TOK, FAR_GROUPS * HEAD_DIM), lambda i: (0, i))
PART = KEY, jax.ShapeDtypeStruct((TOK, KV_HEADS * HEAD_DIM), BF)
FAR_PART = FAR_KEY, PART[1]
OWN = KEY, jax.ShapeDtypeStruct((TOK, KV_HEADS * HEAD_DIM), F32)
QUERY_OUT = QUERY, jax.ShapeDtypeStruct((TOK, KV_HEADS * GROUP * HEAD_DIM), BF)


def call(kernel, in_specs, outs, matmuls, args, scratch=(), steps=KV_HEADS):
    return pl.pallas_call(
        kernel,
        grid=(steps,),
        in_specs=in_specs,
        out_specs=[spec for spec, _ in outs],
        out_shape=[shape for _, shape in outs],
        scratch_shapes=scratch,
        compiler_params=pltpu.CompilerParams(vmem_limit_bytes=VMEM_LIMIT),
        cost_estimate=pl.CostEstimate(
            flops=matmuls * KV_HEADS * 2 * TOK * WIDE * HEAD_DIM, bytes_accessed=2**20, transcendentals=0
        ),
    )(*args)


def probs_of(distance, before, start, q, k):
    own = distance == 0
    return call(
        functools.partial(probs_kernel, distance),
        [SMEM, START, QUERY if own else HELD, KEY],
        [GROUPED] * own + [PROBS, STATS],
        1,
        (before, start, q, k),
    )


def dprobs_of(distance, before, g, v, p):
    own = distance == 0
    return call(
        functools.partial(dprobs_kernel, distance),
        [SMEM, QUERY if own else HELD, KEY, HELD],
        [GROUPED] * own + [DPROBS, STATS],
        1,
        (before, g, v, p),
    )


def far_value(before, start, q4, g4, k, *stats):
    return call(
        far_value_kernel,
        [SMEM, START, HELD, HELD, FAR_KEY, HELD, HELD, HELD],
        [FAR_PART, PROBS, STATS],
        2,
        (before, start, q4, g4, k, *stats),
        [pltpu.VMEM((FAR_GROUPS, 8, WIDE), F32)],
        KV_HEADS // FAR_GROUPS,
    )


def far_key(before, q4, g4, k, v, p, row, *sums):
    return call(
        far_key_kernel,
        [SMEM, HELD, HELD, FAR_KEY, FAR_KEY] + [HELD] * 5,
        [FAR_PART, QUERY_GRAD, STATS],
        3,
        (before, q4, g4, k, v, p, row, *sums),
        [pltpu.VMEM((FAR_GROUPS, TOK, WIDE), F32), pltpu.VMEM((FAR_GROUPS, 8, WIDE), F32)],
        KV_HEADS // FAR_GROUPS,
    )


def value_part(distance, before, g4, p, row):
    return call(
        functools.partial(value_kernel, distance),
        [SMEM, HELD, HELD, HELD],
        [PART if distance else OWN],
        1,
        (before, g4, p, row),
    )[0]


def key_part(distance, before, q4, k, p, dp, row, delta, dq):
    return call(
        functools.partial(key_kernel, distance),
        [SMEM, HELD, KEY] + [HELD] * 5,
        [PART, QUERY_GRAD] if distance else [OWN, QUERY_OUT],
        2,
        (before, q4, k, p, dp, row, delta, dq),
    )


def shift(x, distance):
    devices = range(lax.axis_size(("dp", "ctx")))
    route = [(i - distance, i) for i in devices if i - distance in devices]
    return lax.ppermute(x, ("dp", "ctx"), route)


def add(a, b):
    return (a.astype(F32) + b.astype(F32)).astype(BF)


def after(x, *others):
    return lax.optimization_barrier((x, *others))[0]


def in_hbm(x):
    return pltpu.with_memory_space_constraint(x, pltpu.HBM)


def on_device(queries, keys, values, grad_out, doc_lengths):
    first = lax.axis_index(("dp", "ctx")) * TOK
    ends = jnp.cumsum(doc_lengths)
    pos = first + jnp.arange(TOK, dtype=jnp.int32)
    start = jnp.max(jnp.where(ends[:, None] <= pos[None, :], ends[:, None], 0), axis=0) - first
    before = jnp.maximum(-start[:1], 0)
    start = start[None]
    k, v = [keys], [values]
    k.append(shift(k[0], 1))
    v.append(shift(after(values, start), 1))
    q4, p0, stat0 = probs_of(0, before, start, in_hbm(queries), in_hbm(keys))
    g4, dp0, sum0 = dprobs_of(0, before, in_hbm(grad_out), in_hbm(values), p0)
    p, dp, stat, total = [p0], [dp0], [stat0], [sum0]
    done = sum0
    for d in (1, 2):
        k[d] = after(k[d], done)
        k.append(shift(k[d], 1))
        x, y = probs_of(d, before, start, q4, k[d])
        p.append(x)
        stat.append(y)
        v[d] = after(v[d], y)
        v.append(shift(v[d], 1))
        x, y = dprobs_of(d, before, g4, v[d], p[d])
        dp.append(x)
        total.append(y)
        done = y
    k[3] = after(k[3], done)
    part, p3, row = far_value(before, start, q4, g4, k[3], *stat)
    gv = shift(part, -1)
    v[3] = after(v[3], part)
    part, dq, delta = far_key(before, q4, g4, k[3], v[3], p3, row, *total)
    gk = shift(part, -1)
    done = part
    for d in (2, 1):
        part = value_part(d, before, g4, p[d], after(row, done))
        gv = add(after(gv, part), part)
        done = gv
        gv = shift(gv, -1)
        part, dq = key_part(d, before, q4, k[d], p[d], dp[d], after(row, done), delta, dq)
        gk = add(after(gk, part), part)
        done = gk
        gk = shift(gk, -1)
    own_v = value_part(0, before, g4, p0, after(row, done))
    own_k, grad_queries = key_part(0, before, q4, keys, p0, dp0, after(row, own_v), delta, dq)
    gv = after(gv, own_k)
    return grad_queries, add(own_k, gk), add(own_v, gv)


def solution(mesh):
    spec = P(("dp", "ctx"), None)
    return jax.shard_map(
        on_device,
        mesh=mesh,
        in_specs=(spec, spec, spec, spec, P()),
        out_specs=(spec, spec, spec),
        check_vma=False,
    )
```
